512 devices in a mesh: sec: 2 (over core), seq: 32 (over y, x), tp: 8 (over z).
Axes of the slice: x: 4, y: 8, z: 8, core: 2. Of those that a mesh axis runs over, the one named last changes fastest.
Arguments:
- hidden_rows: bfloat16 [2, 2048, 5120], P('sec', 'seq'), may hold values from -10 to 10
- carried: bfloat16 [2, 2048, 5120], P('sec', 'seq'), may hold values from -6 to 6
- query_weight: bfloat16 [2, 5120, 4096], P('sec', 'seq', 'tp'), may hold values from -6 to 6
- response_cache: bfloat16 [2, 2048, 2048], P('sec', 'seq', 'tp'), may hold values from -8.375 to 8.375
- prompt_cache: bfloat16 [2, 8, 16384, 2048], P('sec', None, 'seq', 'tp'), may hold values from -5 to 5
- prompt_lengths: int32 [8], replicated, may hold values from 1 to 16384, 81920 in all
- response_lengths: int32 [2, 32], replicated, may hold values from 1 to 64, 1280 in all within a row
- block_prompts: int32 [2, 32, 1], replicated, may hold values from 0 to 7
Outputs:
- attended: bfloat16 [2, 2048, 4096], P('sec', 'seq', 'tp')
The draws below stay inside these ranges and needn't reach their ends.
All inputs are finite; a program needn't handle non-finite values.
Results may differ from the reference program's by a relative error of at most 0.0096.
Values may be sent and summed in bfloat16 or wider, within the bound.
A program may use at most 64 MiB of HBM per device.

```python
import math
import jax
import jax.numpy as jnp
import numpy as np
from jax import lax

D = 5120
H = 32
KVH = 8
HD = 128
NP = 8
BL = 64
PL = 16384
GR = 4
NB = 32
ROWS = 2048
N_SEQ = 32


def draw_prompt_cache(key, part):
    key = jax.random.fold_in(key, 5)
    base_key = jax.random.fold_in(key, 0)
    values = jnp.clip(jax.random.normal(base_key, (2, NP, PL, KVH, 2, HD), jnp.float32), -4.5, 4.5)
    return values.reshape(2, NP, PL, KVH * 2 * HD).astype(jnp.bfloat16)


def draw_hidden_rows(key, part):
    key = jax.random.fold_in(key, 9)
    values = jnp.clip(2.6 * jax.random.normal(key, (2, NB, BL, D), jnp.float32), -10.0, 10.0)
    return values.reshape(2, NB * BL, D).astype(jnp.bfloat16)


def draw_carried(key, part):
    key = jax.random.fold_in(key, 11)
    values = jnp.clip(jax.random.normal(key, (2, ROWS, D), jnp.float32), -6.0, 6.0)
    return values.astype(jnp.bfloat16)


def draw_query_weight(key, part):
    key = jax.random.fold_in(key, 13)
    values = jnp.clip(jax.random.normal(key, (2, D, H * HD), jnp.float32), -4.0, 4.0) * D ** (-0.5)
    return values.astype(jnp.bfloat16)


def levels(own_key, extent, cuts, low, high):
    level, own = 1.0, jax.random.fold_in(own_key, 6)
    for axis_at, blocks in cuts:
        steps = jnp.exp(jax.random.uniform(jax.random.fold_in(own, axis_at), (blocks,), jnp.float32, low / len(cuts), high / len(cuts)))
        level = level * jnp.repeat(steps, extent[axis_at] // blocks).reshape([-1 if axis == axis_at else 1 for axis in range(len(extent))])
    return level


def picks_of(own_key, rows, number_of, top, lift):
    order = jax.random.permutation(jax.random.fold_in(own_key, 1), number_of)
    boost = order
    for power in range(3):
        boost = boost * boost // number_of
    boost = boost * lift // number_of
    tickets = jax.random.randint(jax.random.fold_in(own_key, 2), (rows, number_of), 0, 4096) + boost
    sure = jax.random.permutation(jax.random.fold_in(own_key, 3), rows)[jnp.arange(number_of) % rows]
    tickets = jnp.where(jnp.arange(rows)[:, None] == sure[None, :], 1 << 14, tickets)
    score = tickets * number_of + jnp.arange(number_of)
    return lax.top_k(score.astype(jnp.int32), top)[1].astype(jnp.int32)


def length_profile(amount, total, reach, lean):
    portions = [(1 << 20) // math.isqrt(standing ** lean) + 1 for standing in range(2, amount + 1)]
    rest, given = total - reach - (amount - 1), [1] * (amount - 1)
    while rest > 0:
        candidates = [i for i in range(amount - 1) if given[i] < reach]
        pool, left = sum([portions[i] for i in candidates]), rest
        for i in candidates:
            more = min(reach - given[i], max(1, left * portions[i] // pool), rest)
            given[i] = given[i] + more
            rest = rest - more
    return np.array([reach] + given)


def ragged(own_key, number_of, total, bound, lean):
    if number_of == 2:
        one = jax.random.randint(own_key, (), max(1, total - bound), min(bound, total - 1) + 1)
        return jnp.stack([one, total - one])
    tallies = jnp.asarray(length_profile(number_of, total, bound, lean), jnp.int32)
    twos = (number_of - 1) // 2
    giver, sink = tallies[1:1 + 2 * twos:2], tallies[2:2 + 2 * twos:2]
    room = jnp.minimum(giver - 1, bound - sink)
    moved = jax.random.randint(jax.random.fold_in(own_key, 1), (twos,), 0, 1 << 20) % (room + 1)
    tallies = tallies.at[1:1 + 2 * twos:2].set(giver - moved).at[2:2 + 2 * twos:2].set(sink + moved)
    return tallies[jax.random.permutation(jax.random.fold_in(own_key, 2), number_of)]


def noise(rng, extent, deviation, bound, cuts=(), held_as=jnp.bfloat16):
    values = jax.random.normal(rng, extent, jnp.float32) * deviation
    if len(cuts) > 0:
        values = levels(rng, extent, cuts, -0.22, 0.18) * values
    return jnp.clip(values, min=-bound, max=bound).astype(held_as)


def setup_inputs(seed: int = 0) -> dict:
    key_list = jax.random.split(jax.random.key(seed), 9)
    hidden_rows = draw_hidden_rows(jax.random.fold_in(key_list[8], 71), 0)
    carried = draw_carried(jax.random.fold_in(key_list[8], 71), 0)
    query_weight = draw_query_weight(jax.random.fold_in(key_list[8], 71), 0)
    response_cache = noise(key_list[3], (2, ROWS, KVH * 2 * HD), 1.4, 8.375, ((0, 2), (1, 32), (2, 8)))
    prompt_cache = draw_prompt_cache(jax.random.fold_in(key_list[8], 71), 0)
    prompt_lengths = ragged(key_list[5], NP, NP * PL * 5 // 8, PL, 2).astype(jnp.int32)
    response_lengths = jax.vmap(lambda own: ragged(own, NB, NB * BL * 5 // 8, BL, 1))(jax.random.split(key_list[6], 2)).reshape((2, NB)).astype(jnp.int32)
    block_prompts = picks_of(key_list[7], 2 * NB, NP, 1, 2048).reshape((2, NB, 1))
    return dict(hidden_rows=hidden_rows, carried=carried, query_weight=query_weight, response_cache=response_cache, prompt_cache=prompt_cache, prompt_lengths=prompt_lengths, response_lengths=response_lengths, block_prompts=block_prompts)


NEG_FILL = -1e30


def attend_block(query_block, cache_block, response_block, prompt_valid, response_length):
    queries = query_block.astype(jnp.float32)
    prompt_keys = cache_block[:, :, 0].astype(jnp.float32)
    prompt_values = cache_block[:, :, 1].astype(jnp.float32)
    own_keys = response_block[:, :, 0].astype(jnp.float32)
    own_values = response_block[:, :, 1].astype(jnp.float32)
    score_scale = HD ** -0.5
    prompt_scores = jnp.einsum("igqd,jgd->igqj", queries, prompt_keys) * score_scale
    own_scores = jnp.einsum("igqd,tgd->igqt", queries, own_keys) * score_scale
    positions = jnp.arange(BL, dtype=jnp.int32)
    causal = (positions[:, None] >= positions[None, :])[:, None, None, :]
    prompt_mask = prompt_valid[None, None, None, :]
    row_peak = jnp.maximum(
        jnp.max(jnp.where(prompt_mask, prompt_scores, NEG_FILL), axis=-1),
        jnp.max(jnp.where(causal, own_scores, NEG_FILL), axis=-1))
    prompt_weights = jnp.where(prompt_mask, jnp.exp(prompt_scores - row_peak[..., None]), 0.0)
    prompt_weights = lax.optimization_barrier(prompt_weights.astype(jnp.bfloat16)).astype(jnp.float32)
    own_weights = jnp.where(causal, jnp.exp(own_scores - row_peak[..., None]), 0.0)
    own_weights = lax.optimization_barrier(own_weights.astype(jnp.bfloat16)).astype(jnp.float32)
    row_total = jnp.sum(prompt_weights, axis=-1) + jnp.sum(own_weights, axis=-1)
    row_sum = jnp.einsum("igqj,jgd->igqd", prompt_weights, prompt_values)
    row_sum = row_sum + jnp.einsum("igqt,tgd->igqd", own_weights, own_values)
    output = row_sum / row_total[..., None]
    output = jnp.where((positions < response_length)[:, None, None, None], output, 0.0)
    return output.reshape(BL, H * HD).astype(jnp.bfloat16)


def reference(hidden_rows, carried, query_weight, response_cache, prompt_cache, prompt_lengths, response_lengths, block_prompts):
    results = []
    for section in range(2):
        inputs = hidden_rows[section].astype(jnp.float32)
        if section == 1:
            inputs = inputs + carried[0].astype(jnp.float32)
        inputs = inputs.astype(jnp.bfloat16)
        queries = jnp.dot(inputs, query_weight[section], preferred_element_type=jnp.float32)
        queries = queries.astype(jnp.bfloat16).reshape(N_SEQ, BL, KVH, GR, HD)
        responses = response_cache[section].reshape(N_SEQ, BL, KVH, 2, HD)
        caches = prompt_cache[section].reshape(NP, PL, KVH, 2, HD)
        chosen = block_prompts[section, :, 0].astype(jnp.int32)
        lengths = response_lengths[section].astype(jnp.int32)

        def one_block(block_inputs, caches=caches):
            query_block, response_block, prompt_index, response_length = block_inputs
            cache_block = lax.dynamic_index_in_dim(caches, prompt_index, 0, keepdims=False)
            prompt_valid = jnp.arange(PL, dtype=jnp.int32) < prompt_lengths[prompt_index]
            return attend_block(query_block, cache_block, response_block, prompt_valid, response_length)

        blocks = lax.map(one_block, (queries, responses, chosen, lengths))
        results.append(blocks.reshape(N_SEQ * BL, H * HD))
    return jnp.stack(results)
```

```python
import jax
import jax.numpy as jnp
from jax import lax
from jax.experimental import pallas as pl
from jax.experimental.pallas import tpu as pltpu
from jax.sharding import PartitionSpec as P

MESH = pl.DeviceIdType.MESH
HD = 128
NP = 8
TILE = 512
NX, NY = 4, 8
BL = 64
DEPTH = 160
WIDE = DEPTH * NY
COLS = 512
LANES = 256
HALF = 128
PAY = 144
SUB = DEPTH // 2
NEG = -1e30
SCALE = HD**-0.5 * 1.4426950408889634
F32 = jnp.float32
BF16 = jnp.bfloat16


def slot(rx, ry):
    return lax.rem(ry + NY, NY) * NX + rx if not isinstance(ry, int) else (ry % NY) * NX + rx


def kernel(
    bp,
    plen,
    rlen,
    hid_h,
    car_h,
    w_h,
    rc_h,
    kv_h,
    out,
    hid,
    handed,
    xin,
    lhs,
    wbuf,
    pbuf,
    prec,
    kv,
    rc,
    vt,
    q,
    own,
    mine,
    send_a,
    send_b,
    ra_y,
    ra_x,
    rb_y,
    rb_x,
    local_sem,
    hand_s,
    hand_r,
    xin_s,
    xin_r,
    w_s,
    w_r,
    p_s,
    p_r,
    qay_s,
    qay_r,
    qax_s,
    qax_r,
    qby_s,
    qby_r,
    qbx_s,
    qbx_r,
    oay_s,
    oay_r,
    oax_s,
    oax_r,
    oby_s,
    oby_r,
    obx_s,
    obx_r,
):
    sec = lax.axis_index("sec")
    seq = lax.axis_index("seq")
    y, x = seq // NX, lax.rem(seq, NX)
    turn = 1 - 2 * sec

    def at_x(rx):
        return lax.rem(x + turn * rx + 2 * NX, NX)

    def at_y(ry):
        return lax.rem(y + turn * ry + 2 * NY, NY)

    def dev(rx, ry):
        return at_y(ry) * NX + at_x(rx)

    xp, xm, x2 = dev(1, 0), dev(-1, 0), dev(2, 0)
    yp, ym = dev(0, 1), dev(0, -1)
    drains = []

    def copy(src, dst, ss, rs, where):
        return pltpu.make_async_remote_copy(
            src_ref=src,
            dst_ref=dst,
            send_sem=ss,
            recv_sem=rs,
            device_id={"seq": where},
            device_id_type=MESH,
        )

    def push(src, dst, ss, rs, where):
        c = copy(src, dst, ss, rs, where)
        c.start()
        drains.append(c.wait_send)

    def got(dst, rs):
        copy(dst, dst, rs, rs, xp).wait_recv()

    in_hid = pltpu.make_async_copy(hid_h.at[0], hid, local_sem.at[0])
    in_kv = pltpu.make_async_copy(kv_h.at[0], kv, local_sem.at[1])
    in_rc = pltpu.make_async_copy(rc_h.at[0], rc, local_sem.at[2])
    in_w = pltpu.make_async_copy(w_h.at[0], wbuf.at[y], local_sem.at[3])
    in_hid.start()
    in_w.start()
    in_kv.start()
    in_rc.start()

    barrier = pltpu.get_barrier_semaphore()
    for where in (xp, xm, x2, yp, ym):
        pl.semaphore_signal(barrier, inc=1, device_id={"seq": where}, device_id_type=MESH)
    pl.semaphore_signal(barrier, inc=1, device_id={"sec": 1 - sec}, device_id_type=MESH)
    pl.semaphore_wait(barrier, 6)

    hand = pltpu.make_async_remote_copy(
        src_ref=car_h.at[0],
        dst_ref=handed,
        send_sem=hand_s,
        recv_sem=hand_r,
        device_id={"sec": 1 - sec},
        device_id_type=MESH,
    )

    @pl.when(sec == 0)
    def _():
        hand.start()

    def w_part(ry, sub):
        return wbuf.at[at_y(ry), pl.ds(sub * SUB, SUB), :]

    for sub in range(2):
        part = w_h.at[0, pl.ds(sub * SUB, SUB), :]
        push(part, w_part(0, sub), w_s.at[0, 0, sub], w_r.at[0, 0, sub], yp)
        push(part, w_part(0, sub), w_s.at[1, 0, sub], w_r.at[1, 0, sub], ym)

    @pl.when(sec == 0)
    def _():
        handed[...] = jnp.zeros_like(handed)

    @pl.when(sec == 1)
    def _():
        hand.wait_recv()

    in_hid.wait()

    def regroup(r, carry):
        rows = pl.ds(pl.multiple_of(r * 16, 16), 16)
        lane = lax.broadcasted_iota(jnp.int32, (16, 4 * DEPTH), 1)
        for g in range(2):
            parts = []
            for j in range(4):
                cols = pl.ds(4 * DEPTH * (4 * g + j), 4 * DEPTH)
                v = hid[rows, cols].astype(F32) + handed[rows, cols].astype(F32)
                parts.append(v.astype(BF16).astype(F32))
            for xx in range(NX):
                total = None
                for j in range(4):
                    shift = (DEPTH * (j - xx)) % (4 * DEPTH)
                    v = parts[j] if shift == 0 else pltpu.roll(parts[j], shift, 1)
                    total = v if total is None else jnp.where(lane >= DEPTH * j, v, total)
                xin[xx, rows, pl.ds(4 * DEPTH * g, 4 * DEPTH)] = total.astype(BF16)
        return carry

    lax.fori_loop(0, BL // 16, regroup, 0)
    for n, (rx, where) in enumerate(((1, xp), (-1, xm), (2, x2))):
        push(xin.at[at_x(rx)], lhs.at[(-rx) % NX], xin_s.at[n], xin_r.at[n], where)
    lhs[0] = xin[x]

    in_kv.wait()

    def values_across(p, carry):
        vt[p, 0:HD, :] = kv[p, :, HD : 2 * HD].astype(F32).T.astype(BF16)
        vt[p, HD:PAY, :] = jnp.ones((PAY - HD, TILE), BF16)
        return carry

    for k in range(1, 5):
        for sub in range(2):
            got(w_part(-k, sub), w_r.at[0, k - 1, sub])
            if k < 4:
                part = w_part(-k, sub)
                push(part, part, w_s.at[0, k, sub], w_r.at[0, k, sub], yp)
                got(w_part(k, sub), w_r.at[1, k - 1, sub])
                if k < 3:
                    part = w_part(k, sub)
                    push(part, part, w_s.at[1, k, sub], w_r.at[1, k, sub], ym)
        if k < 4:
            lax.fori_loop(3 * k - 3, min(3 * k, NP), values_across, 0)

    in_w.wait()
    in_rc.wait()
    got(lhs.at[2], xin_r.at[2])
    got(lhs.at[3], xin_r.at[0])
    weight = wbuf[...].reshape(WIDE, COLS)
    far = jnp.dot(lhs[2:4].reshape(2 * BL, WIDE), weight, preferred_element_type=F32)
    pbuf[2:4] = far.reshape(2, BL, COLS)
    push(pbuf.at[2], prec.at[0], p_s.at[0], p_r.at[0], xp)
    push(pbuf.at[3], prec.at[2], p_s.at[2], p_r.at[2], xm)
    got(lhs.at[1], xin_r.at[1])
    near = jnp.dot(lhs[0:2].reshape(2 * BL, WIDE), weight, preferred_element_type=F32)
    pbuf[0:2] = near.reshape(2, BL, COLS)
    got(prec.at[0], p_r.at[0])
    pbuf[1] = pbuf[1] + prec[0]
    push(pbuf.at[1], prec.at[1], p_s.at[1], p_r.at[1], xp)
    got(prec.at[2], p_r.at[2])
    got(prec.at[1], p_r.at[1])
    mine_q = pbuf[0] + prec[1] + prec[2]
    for h in range(2):
        first = mine_q[:, 2 * h * HD : (2 * h + 1) * HD]
        second = mine_q[:, (2 * h + 1) * HD : (2 * h + 2) * HD]
        both = jnp.concatenate([first, second], axis=0)
        q[0, :, h * HALF : (h + 1) * HALF] = both.T.astype(BF16)

    def q_a(s):
        return q.at[s, :, pl.ds(0, HALF)]

    def q_b(s):
        return q.at[s, :, pl.ds(HALF, HALF)]

    def a_hop(arm, k, i):
        sign = -1 if arm == 0 else 1
        src, dst = slot(i, sign * (k - 1)), slot(i, sign * k)
        return copy(
            q_a(src),
            q_a(dst),
            qay_s.at[arm, k - 1, i],
            qay_r.at[arm, k - 1, i],
            yp if arm == 0 else ym,
        )

    def b_hop(arm, k):
        sign = -1 if arm == 0 else 1
        return copy(
            q_b(slot(0, sign * (k - 1))),
            q_b(slot(0, sign * k)),
            qby_s.at[arm, k - 1],
            qby_r.at[arm, k - 1],
            yp if arm == 0 else ym,
        )

    def b_side(n, ry):
        src, dst = ((0, 3), (0, 1), (3, 2))[n]
        return copy(
            q_b(slot(src, ry)),
            q_b(slot(dst, ry)),
            qbx_s.at[n, ry % NY],
            qbx_r.at[n, ry % NY],
            xm if n == 1 else xp,
        )

    def go(c):
        c.start()
        drains.append(c.wait_send)

    a_side = [
        copy(q_a(0), q_a(3), qax_s.at[0], qax_r.at[0], xp),
        copy(q_a(0), q_a(1), qax_s.at[1], qax_r.at[1], xm),
        copy(q_a(0), q_a(2), qax_s.at[2], qax_r.at[2], x2),
    ]
    for c in a_side:
        go(c)
    go(b_hop(0, 1))
    go(b_hop(1, 1))
    go(a_hop(0, 1, 0))
    go(a_hop(1, 1, 0))
    go(b_side(0, 0))
    go(b_side(1, 0))

    own_s = (
        jnp.dot(rc[:, 0:HD], q[0], preferred_element_type=F32) * SCALE
    )
    own_t = lax.broadcasted_iota(jnp.int32, (BL, LANES), 0)
    own_i = lax.rem(lax.broadcasted_iota(jnp.int32, (BL, LANES), 1), BL)
    own_s = jnp.where(own_t <= own_i, own_s, NEG)
    own_m = jnp.max(own_s, axis=0, keepdims=True)
    own_w = jnp.exp2(own_s - own_m).astype(BF16)
    own_v = rc[:, HD : 2 * HD].astype(F32).T.astype(BF16)
    mine[0:HD] = jnp.dot(own_v, own_w, preferred_element_type=F32)
    mine[HD : HD + 8] = jnp.broadcast_to(
        jnp.sum(own_w.astype(F32), axis=0, keepdims=True), (8, LANES)
    )
    mine[HD + 8 : PAY] = jnp.broadcast_to(own_m, (8, LANES))

    for c, i in ((a_side[1], 1), (a_side[2], 2), (a_side[0], 3)):
        c.wait_recv()
        go(a_hop(0, 1, i))
        go(a_hop(1, 1, i))
    b_side(0, 0).wait_recv()
    go(b_side(2, 0))

    def attend(rx, ry):
        s = slot(rx, ry)
        block = at_y(ry) * NX + at_x(rx)
        p = bp[sec * (NX * NY) + block]
        valid = plen[p] - seq * TILE
        scores = jnp.dot(kv[p, :, 0:HD], q[s], preferred_element_type=F32) * SCALE
        place = lax.broadcasted_iota(jnp.int32, (TILE, LANES), 0)
        scores = jnp.where(place < valid, scores, NEG)
        peak = jnp.max(scores, axis=0, keepdims=True)
        shift = jnp.where(valid > 0, peak, 0.0)
        weights = jnp.exp2(scores - shift).astype(BF16)
        own[s] = jnp.dot(vt[p], weights, preferred_element_type=F32)
        own[s, HD + 8 : PAY] = jnp.broadcast_to(peak, (8, LANES))

    for k in range(1, 6):
        if k <= 4:
            b_hop(0, k).wait_recv()
            if k < 4:
                go(b_hop(0, k + 1))
            go(b_side(0, -k))
            go(b_side(1, -k))
        if k <= 3:
            b_hop(1, k).wait_recv()
            if k < 3:
                go(b_hop(1, k + 1))
            go(b_side(0, k))
            go(b_side(1, k))
        signs = (1,) if k in (1, 5) else (1, -1)

        def blocks(i, carry, k=k, signs=signs):
            if k <= 4:
                a_hop(0, k, i).wait_recv()
                if k < 4:
                    a_hop(0, k + 1, i).start()
            if k <= 3:
                a_hop(1, k, i).wait_recv()
                if k < 3:
                    a_hop(1, k + 1, i).start()
            rx = i + (i // 2) * (1 - 2 * lax.rem(i, 2))
            for sign in signs:
                ry = sign * (k - 1)

                @pl.when(rx == 1)
                def _():
                    b_side(1, ry).wait_recv()

                @pl.when(rx == 2)
                def _():
                    b_side(2, ry).wait_recv()

                attend(rx, ry)
            return carry

        lax.fori_loop(0, NX, blocks, 0)
        if k <= 4:
            b_side(0, -k).wait_recv()
            go(b_side(2, -k))
        if k <= 3:
            b_side(0, k).wait_recv()
            go(b_side(2, k))

    def part_of(ref, h):
        cols = pl.ds(h * HALF, HALF)
        return ref[0:HD, cols], ref[HD : HD + 1, cols], ref[HD + 8 : HD + 9, cols]

    def arrived(ref):
        st = ref[HD:PAY].astype(F32)
        total = st[0:1] + st[1:2] + st[2:3]
        peak = st[8:9] + st[9:10] + st[10:11]
        return ref[0:HD].astype(F32), total, peak

    def merge(*parts):
        peak = parts[0][2]
        for part in parts[1:]:
            peak = jnp.maximum(peak, part[2])
        sums, total = None, None
        for o, l, m in parts:
            scale = jnp.exp2(m - peak)
            sums = o * scale if sums is None else sums + o * scale
            total = l * scale if total is None else total + l * scale
        return sums, total, peak

    def put(ref, part):
        o, l, m = part
        ref[0:HD] = o.astype(BF16)
        row = lax.broadcasted_iota(jnp.int32, (PAY - HD, HALF), 0)
        v = jnp.where(row < 8, l, m)
        high = v.astype(BF16).astype(F32)
        rest = v - high
        mid = rest.astype(BF16).astype(F32)
        low = rest - mid
        sub = lax.rem(row, 8)
        ref[HD:PAY] = jnp.where(sub == 0, high, jnp.where(sub == 1, mid, low)).astype(BF16)

    def oa_hop(arm, k, i):
        sign = 1 if arm == 0 else -1
        return copy(
            send_a.at[slot(i, sign * k)],
            ra_y.at[arm, k - 1, i],
            oay_s.at[arm, k - 1, i],
            oay_r.at[arm, k - 1, i],
            yp if arm == 0 else ym,
        )

    def ob_hop(arm, k):
        sign = 1 if arm == 0 else -1
        return copy(
            send_b.at[slot(0, sign * k)],
            rb_y.at[arm, k - 1],
            oby_s.at[arm, k - 1],
            oby_r.at[arm, k - 1],
            yp if arm == 0 else ym,
        )

    def ob_side(n, ry):
        return copy(
            send_b.at[slot((2, 1, 3)[n], ry)],
            rb_x.at[n, ry % NY],
            obx_s.at[n, ry % NY],
            obx_r.at[n, ry % NY],
            xm if n == 2 else xp,
        )

    def oa_side(n):
        return copy(
            send_a.at[slot((2, 1, 3)[n], 0)],
            ra_x.at[n],
            oax_s.at[n],
            oax_r.at[n],
            xm if n == 2 else xp,
        )

    def side_first(ry):
        put(send_b.at[slot(2, ry)], part_of(own.at[slot(2, ry)], 1))
        go(ob_side(0, ry))
        put(send_b.at[slot(3, ry)], part_of(own.at[slot(3, ry)], 1))
        go(ob_side(2, ry))

    def side_second(ry):
        ob_side(0, ry).wait_recv()
        put(
            send_b.at[slot(1, ry)],
            merge(part_of(own.at[slot(1, ry)], 1), arrived(rb_x.at[0, ry % NY])),
        )
        go(ob_side(1, ry))

    def side_last(ry):
        ob_side(2, ry).wait_recv()
        ob_side(1, ry).wait_recv()
        parts = [
            part_of(own.at[slot(0, ry)], 1),
            arrived(rb_x.at[1, ry % NY]),
            arrived(rb_x.at[2, ry % NY]),
        ]
        k = abs(ry)
        arm = 0 if ry > 0 else 1
        if k < (4 if arm == 0 else 3):
            ob_hop(arm, k + 1).wait_recv()
            parts.append(arrived(rb_y.at[arm, k]))
        put(send_b.at[slot(0, ry)], merge(*parts))
        go(ob_hop(arm, k))

    side_first(4)
    side_first(3)
    side_first(-3)
    for k in range(4, 0, -1):
        if k < 4:
            for ry in (k + 1, -k - 1):
                if ry != -4:
                    side_last(ry)

        def back(i, carry, k=k):
            for arm in range(2):
                if arm == 1 and k == 4:
                    continue
                s = slot(i, k if arm == 0 else -k)
                part = part_of(own.at[s], 0)
                if k < 4 - arm:
                    oa_hop(arm, k + 1, i).wait_recv()
                    part = merge(part, arrived(ra_y.at[arm, k, i]))
                put(send_a.at[s], part)
                oa_hop(arm, k, i).start()
            return carry

        lax.fori_loop(0, NX, back, 0)
        for ry in (k, -k):
            if ry != -4:
                side_second(ry)
        for ry in (k - 2, 2 - k):
            if k >= 3:
                side_first(ry)
        if k == 2:
            side_first(0)

    side_last(1)
    side_last(-1)

    def a_here(i):
        oa_hop(0, 1, i).wait_recv()
        oa_hop(1, 1, i).wait_recv()
        return [
            part_of(own.at[slot(i, 0)], 0),
            arrived(ra_y.at[0, 0, i]),
            arrived(ra_y.at[1, 0, i]),
        ]

    put(send_a.at[slot(2, 0)], merge(*a_here(2)))
    go(oa_side(0))
    put(send_a.at[slot(3, 0)], merge(*a_here(3)))
    go(oa_side(2))
    side_second(0)
    a_one = a_here(1)
    oa_side(0).wait_recv()
    put(send_a.at[slot(1, 0)], merge(*a_one, arrived(ra_x.at[0])))
    go(oa_side(1))

    lane_i = lax.rem(lax.broadcasted_iota(jnp.int32, (1, HALF), 1), BL)
    kept = lane_i < rlen[sec * (NX * NY) + seq]

    def finish(h, parts):
        o, l, _ = merge(part_of(mine, h), *parts)
        rows = jnp.where(kept, o / l, 0.0).T
        out[0, :, 2 * h * HD : (2 * h + 1) * HD] = rows[0:BL].astype(BF16)
        out[0, :, (2 * h + 1) * HD : (2 * h + 2) * HD] = rows[BL : 2 * BL].astype(BF16)

    ob_side(2, 0).wait_recv()
    ob_side(1, 0).wait_recv()
    ob_hop(0, 1).wait_recv()
    ob_hop(1, 1).wait_recv()
    finish(
        1,
        [part_of(own.at[0], 1)]
        + [arrived(r) for r in (rb_x.at[1, 0], rb_x.at[2, 0], rb_y.at[0, 0], rb_y.at[1, 0])],
    )
    a_zero = a_here(0)
    oa_side(2).wait_recv()
    oa_side(1).wait_recv()
    finish(0, a_zero + [arrived(ra_x.at[1]), arrived(ra_x.at[2])])

    for done in drains:
        done()

    def rest(i, carry):
        for k in range(2, 5):
            a_hop(0, k, i).wait_send()
            if k < 4:
                a_hop(1, k, i).wait_send()
        for k in range(1, 5):
            oa_hop(0, k, i).wait_send()
            if k < 4:
                oa_hop(1, k, i).wait_send()
        return carry

    lax.fori_loop(0, NX, rest, 0)

    @pl.when(sec == 0)
    def _():
        hand.wait_send()


def shards(hidden, carried, weight, responses, prompts, prompt_lengths, response_lengths, block_prompts):
    any_space = pl.BlockSpec(memory_space=pl.ANY)
    scalars = pl.BlockSpec(memory_space=pltpu.SMEM)
    dma = pltpu.SemaphoreType.DMA
    vmem = pltpu.VMEM
    sems = [
        (4,),
        None,
        None,
        (3,),
        (3,),
        (2, 4, 2),
        (2, 4, 2),
        (3,),
        (3,),
        (2, 4, NX),
        (2, 4, NX),
        (3,),
        (3,),
        (2, 4),
        (2, 4),
        (3, NY),
        (3, NY),
        (2, 4, NX),
        (2, 4, NX),
        (3,),
        (3,),
        (2, 4),
        (2, 4),
        (3, NY),
        (3, NY),
    ]
    return pl.pallas_call(
        kernel,
        out_shape=jax.ShapeDtypeStruct((1, BL, COLS), BF16),
        in_specs=[scalars] * 3 + [any_space] * 5,
        out_specs=pl.BlockSpec(memory_space=pltpu.VMEM),
        scratch_shapes=[
            vmem((BL, 4 * WIDE), BF16),
            vmem((BL, 4 * WIDE), BF16),
            vmem((NX, BL, WIDE), BF16),
            vmem((NX, BL, WIDE), BF16),
            vmem((NY, DEPTH, COLS), BF16),
            vmem((NX, BL, COLS), F32),
            vmem((3, BL, COLS), F32),
            vmem((NP, TILE, 2 * HD), BF16),
            vmem((BL, 2 * HD), BF16),
            vmem((NP, PAY, TILE), BF16),
            vmem((NX * NY, HD, LANES), BF16),
            vmem((NX * NY, PAY, LANES), F32),
            vmem((PAY, LANES), F32),
            vmem((NX * NY, PAY, HALF), BF16),
            vmem((NX * NY, PAY, HALF), BF16),
            vmem((2, 4, NX, PAY, HALF), BF16),
            vmem((3, PAY, HALF), BF16),
            vmem((2, 4, PAY, HALF), BF16),
            vmem((3, NY, PAY, HALF), BF16),
        ]
        + [dma if s is None else dma(s) for s in sems],
        compiler_params=pltpu.CompilerParams(
            collective_id=0, has_side_effects=True, vmem_limit_bytes=48 << 20
        ),
    )(
        block_prompts.reshape(-1),
        prompt_lengths,
        response_lengths.reshape(-1),
        hidden,
        carried,
        weight,
        responses,
        prompts,
    )


def solution(mesh):
    placed = (
        P("sec", "seq", None),
        P("sec", "seq", None),
        P("sec", "seq", "tp"),
        P("sec", "seq", "tp"),
        P("sec", None, "seq", "tp"),
        P(),
        P(),
        P(),
    )
    return jax.shard_map(
        shards, mesh=mesh, in_specs=placed, out_specs=P("sec", "seq", "tp"), check_vma=False
    )
```

```python
import jax
import jax.numpy as jnp
from jax import lax
from jax.experimental import pallas as pl
from jax.experimental.pallas import tpu as pltpu
from jax.sharding import PartitionSpec as P

MESH = pl.DeviceIdType.MESH
HD = 128
NP = 8
TILE = 512
NX, NY = 4, 8
BL = 64
DEPTH = 160
WIDE = DEPTH * NY
COLS = 512
LANES = 256
HALF = 128
PAY = 144
SUB = DEPTH // 2
NEG = -1e30
SCALE = HD**-0.5 * 1.4426950408889634
F32 = jnp.float32
BF16 = jnp.bfloat16


def slot(rx, ry):
    return lax.rem(ry + NY, NY) * NX + rx if not isinstance(ry, int) else (ry % NY) * NX + rx


def kernel(
    bp,
    plen,
    rlen,
    hid_h,
    car_h,
    w_h,
    rc_h,
    kv_h,
    out,
    hid,
    handed,
    xin,
    lhs,
    transit,
    wbuf,
    pbuf,
    prec,
    kv,
    rc,
    vt,
    q,
    own,
    mine,
    back,
    from_y,
    from_x,
    local_sem,
    hand_s,
    hand_r,
    xin_s,
    xin_r,
    w_s,
    w_r,
    p_s,
    p_r,
    qy_s,
    qy_r,
    qx_s,
    qx_r,
    oy_s,
    oy_r,
    ox_s,
    ox_r,
):
    sec = lax.axis_index("sec")
    seq = lax.axis_index("seq")
    y, x = seq // NX, lax.rem(seq, NX)
    turn = 1 - 2 * sec

    def at_x(rx):
        return lax.rem(x + turn * rx + 2 * NX, NX)

    def at_y(ry):
        return lax.rem(y + turn * ry + 2 * NY, NY)

    def dev(rx, ry):
        return at_y(ry) * NX + at_x(rx)

    xp, xm, x2 = dev(1, 0), dev(-1, 0), dev(2, 0)
    yp, ym = dev(0, 1), dev(0, -1)
    drains = []

    def copy(src, dst, ss, rs, where):
        return pltpu.make_async_remote_copy(
            src_ref=src,
            dst_ref=dst,
            send_sem=ss,
            recv_sem=rs,
            device_id={"seq": where},
            device_id_type=MESH,
        )

    def push(src, dst, ss, rs, where):
        c = copy(src, dst, ss, rs, where)
        c.start()
        drains.append(c.wait_send)

    def got(dst, rs):
        copy(dst, dst, rs, rs, xp).wait_recv()

    in_hid = pltpu.make_async_copy(hid_h.at[0], hid, local_sem.at[0])
    in_kv = pltpu.make_async_copy(kv_h.at[0], kv, local_sem.at[1])
    in_rc = pltpu.make_async_copy(rc_h.at[0], rc, local_sem.at[2])
    in_w = pltpu.make_async_copy(w_h.at[0], wbuf.at[y], local_sem.at[3])
    in_hid.start()
    in_w.start()
    in_kv.start()
    in_rc.start()

    barrier = pltpu.get_barrier_semaphore()
    for where in (xp, xm, x2, yp, ym):
        pl.semaphore_signal(barrier, inc=1, device_id={"seq": where}, device_id_type=MESH)

    @pl.when(sec == 1)
    def _():
        pl.semaphore_signal(barrier, inc=1, device_id={"sec": 0}, device_id_type=MESH)
        pl.semaphore_wait(barrier, 5)

    @pl.when(sec == 0)
    def _():
        pl.semaphore_wait(barrier, 6)

    hand = pltpu.make_async_remote_copy(
        src_ref=car_h.at[0],
        dst_ref=handed,
        send_sem=hand_s,
        recv_sem=hand_r,
        device_id={"sec": 1},
        device_id_type=MESH,
    )

    @pl.when(sec == 0)
    def _():
        hand.start()

    wide = COLS // 2

    def w_part(ry, h, r):
        return wbuf.at[at_y(ry), pl.ds(r * SUB, SUB), pl.ds(h * wide, wide)]

    def w_hop(arm, k, h, r):
        sign = -1 if arm == 0 else 1
        part = w_part(sign * (k - 1), h, r)
        src = w_h.at[0, pl.ds(r * SUB, SUB), pl.ds(h * wide, wide)] if k == 1 else part
        where = yp if arm == 0 else ym
        return copy(src, part, w_s.at[arm, k - 1, h, r], w_r.at[arm, k - 1, h, r], where)

    def go(c):
        c.start()
        drains.append(c.wait_send)

    def w_on(k, h):
        for r in range(2):
            for arm in range(2):
                if k <= 4 - arm:
                    if k > 0:
                        got(w_part((-k, k)[arm], h, r), w_r.at[arm, k - 1, h, r])
                    if k < 4 - arm:
                        go(w_hop(arm, k + 1, h, r))

    w_on(0, 0)
    w_on(0, 1)

    rows_of = [pl.ds(r * (BL // 2), BL // 2) for r in range(2)]
    far_out = [
        copy(xin.at[at_x(2), rows], transit.at[rows], xin_s.at[2, r], xin_r.at[2, r], xp)
        for r, rows in enumerate(rows_of)
    ]
    far_on = [
        copy(transit.at[rows], lhs.at[2, rows], xin_s.at[3, r], xin_r.at[3, r], xp)
        for r, rows in enumerate(rows_of)
    ]
    near_out = [
        copy(xin.at[at_x(-1)], lhs.at[1], xin_s.at[1, 0], xin_r.at[1, 0], xm),
        copy(xin.at[at_x(1)], lhs.at[3], xin_s.at[0, 0], xin_r.at[0, 0], xp),
    ]

    def regroup(with_handed):
        def rows16(r, carry):
            rows = pl.ds(pl.multiple_of(r * 16, 16), 16)
            lane = lax.broadcasted_iota(jnp.int32, (16, 4 * DEPTH), 1)
            for g in range(2):
                parts = []
                for j in range(4):
                    cols = pl.ds(4 * DEPTH * (4 * g + j), 4 * DEPTH)
                    v = hid[rows, cols].astype(F32)
                    if with_handed:
                        v = v + handed[rows, cols].astype(F32)
                        v = v.astype(BF16).astype(F32)
                    parts.append(v)
                for xx in range(NX):
                    total = None
                    for j in range(4):
                        shift = (DEPTH * (j - xx)) % (4 * DEPTH)
                        v = parts[j] if shift == 0 else pltpu.roll(parts[j], shift, 1)
                        total = v if total is None else jnp.where(lane >= DEPTH * j, v, total)
                    xin[xx, rows, pl.ds(4 * DEPTH * g, 4 * DEPTH)] = total.astype(BF16)
            return carry

        lax.fori_loop(0, BL // 16, rows16, 0)

    def values_across(p, carry):
        vt[p, 0:HD, :] = kv[p, :, HD : 2 * HD].astype(F32).T.astype(BF16)
        vt[p, HD:PAY, :] = jnp.ones((PAY - HD, TILE), BF16)
        return carry

    in_hid.wait()

    @pl.when(sec == 0)
    def _():
        regroup(False)

    @pl.when(sec == 1)
    def _():
        hand.wait_recv()
        regroup(True)

    for c in (*far_out, *near_out):
        go(c)
    lhs[0] = xin[x]
    w_on(1, 0)
    w_on(2, 0)
    w_on(1, 1)
    for come, on_c in zip(far_out, far_on):
        come.wait_recv()
        go(on_c)
    in_kv.wait()
    lax.fori_loop(0, 3, values_across, 0)
    w_on(3, 0)
    w_on(2, 1)
    lax.fori_loop(3, 5, values_across, 0)
    w_on(4, 0)

    in_w.wait()
    in_rc.wait()
    for c in (*near_out, *far_on):
        c.wait_recv()

    def heads(ref, n, h):
        return ref.at[n, :, pl.ds(h * wide, wide)]

    def partial(first, h):
        rows = jnp.dot(
            lhs[first : first + 2].reshape(2 * BL, WIDE),
            wbuf[:, :, h * wide : (h + 1) * wide].reshape(WIDE, wide),
            preferred_element_type=F32,
        )
        pbuf[first : first + 2, :, h * wide : (h + 1) * wide] = rows.reshape(2, BL, wide)

    def send_partial(src, dst, h, where):
        push(heads(pbuf, src, h), heads(prec, dst, h), p_s.at[dst, h], p_r.at[dst, h], where)

    def partials(h):
        partial(2, h)
        send_partial(2, 0, h, xp)
        send_partial(3, 2, h, xm)
        partial(0, h)

    def add_far(h):
        cols = slice(h * wide, (h + 1) * wide)
        got(heads(prec, 0, h), p_r.at[0, h])
        pbuf[1, :, cols] = pbuf[1, :, cols] + prec[0, :, cols]
        send_partial(1, 1, h, xp)

    def my_queries(h):
        cols = slice(h * wide, (h + 1) * wide)
        got(heads(prec, 2, h), p_r.at[2, h])
        got(heads(prec, 1, h), p_r.at[1, h])
        mine_q = pbuf[0, :, cols] + prec[1, :, cols] + prec[2, :, cols]
        both = jnp.concatenate([mine_q[:, 0:HD], mine_q[:, HD : 2 * HD]], axis=0)
        q[0, :, h * HALF : (h + 1) * HALF] = both.T.astype(BF16)

    def half(s, h):
        return q.at[s, :, pl.ds(h * HALF, HALF)]

    def y_out(arm, k, h, i):
        sign = -1 if arm == 0 else 1
        return copy(
            half(slot(i, sign * (k - 1)), h),
            half(slot(i, sign * k), h),
            qy_s.at[arm, k - 1, h, i],
            qy_r.at[arm, k - 1, h, i],
            yp if arm == 0 else ym,
        )

    x_side = [
        [
            copy(half(0, h), half(dst, h), qx_s.at[dst - 1, h], qx_r.at[dst - 1, h], where)
            for dst, where in ((1, xm), (3, xp), (2, x2))
        ]
        for h in range(2)
    ]

    def on(k, h, *columns):
        for i in columns or (0, 1, 3, 2):
            for arm in range(2):
                if k <= 4 - arm:
                    if k > 0:
                        y_out(arm, k, h, i).wait_recv()
                    if k < 4 - arm:
                        go(y_out(arm, k + 1, h, i))

    def row_of(h):
        my_queries(h)
        for c in x_side[h]:
            go(c)
        on(0, h, 0)

    def row_on(h):
        for c, i in zip(x_side[h], (1, 3, 2)):
            c.wait_recv()
            on(0, h, i)

    def attend(ry):
        spots = [slot(rx, ry) for rx in range(NX)]
        prompts = [bp[sec, 0, at_y(ry) * NX + at_x(rx)] for rx in range(NX)]
        valid = [plen[p] - seq * TILE for p in prompts]
        place = lax.broadcasted_iota(jnp.int32, (TILE, LANES), 0)
        scores = []
        for s, p, v in zip(spots, prompts, valid):
            raw = jnp.dot(kv[p, :, 0:HD], q[s], preferred_element_type=F32)
            scores.append(jnp.where(place < v, raw * SCALE, NEG))
        weights = []
        for s, v, score in zip(spots, valid, scores):
            peak = jnp.max(score, axis=0, keepdims=True)
            shift = jnp.where(v > 0, peak, 0.0)
            weights.append((peak, jnp.exp2(score - shift).astype(BF16)))
        for s, p, (peak, w) in zip(spots, prompts, weights):
            own[s] = jnp.dot(vt[p], w, preferred_element_type=F32)
            own[s, HD + 8 : PAY] = jnp.broadcast_to(peak, (8, LANES))

    partials(0)
    w_on(3, 1)
    add_far(0)
    lax.fori_loop(5, NP, values_across, 0)
    w_on(4, 1)
    partials(1)
    row_of(0)
    add_far(1)
    row_on(0)
    row_of(1)
    on(1, 0)

    own_s = jnp.dot(rc[:, 0:HD], q[0], preferred_element_type=F32) * SCALE
    own_t = lax.broadcasted_iota(jnp.int32, (BL, LANES), 0)
    own_i = lax.rem(lax.broadcasted_iota(jnp.int32, (BL, LANES), 1), BL)
    own_s = jnp.where(own_t <= own_i, own_s, NEG)
    own_m = jnp.max(own_s, axis=0, keepdims=True)
    own_w = jnp.exp2(own_s - own_m).astype(BF16)
    own_v = rc[:, HD : 2 * HD].astype(F32).T.astype(BF16)
    mine[0:HD] = jnp.dot(own_v, own_w, preferred_element_type=F32)
    mine[HD : HD + 8] = jnp.broadcast_to(
        jnp.sum(own_w.astype(F32), axis=0, keepdims=True), (8, LANES)
    )
    mine[HD + 8 : PAY] = jnp.broadcast_to(own_m, (8, LANES))

    def widths(ry):
        return (slice(0, HALF), slice(HALF, LANES)) if abs(ry) > 2 else (slice(0, LANES),)

    def part_of(ref, cols):
        return ref[0:HD, cols], ref[HD : HD + 1, cols], ref[HD + 8 : HD + 9, cols]

    def arrived(ref, cols):
        st = ref[HD:PAY, cols].astype(F32)
        total = st[0:1] + st[1:2] + st[2:3]
        peak = st[8:9] + st[9:10] + st[10:11]
        return ref[0:HD, cols].astype(F32), total, peak

    def merge(*parts):
        peak = parts[0][2]
        for part in parts[1:]:
            peak = jnp.maximum(peak, part[2])
        sums, total = None, None
        for o, l, m in parts:
            scale = jnp.exp2(m - peak)
            sums = o * scale if sums is None else sums + o * scale
            total = l * scale if total is None else total + l * scale
        return sums, total, peak

    def put(s, cols, part):
        o, l, m = part
        back[s, 0:HD, cols] = o.astype(BF16)
        row = lax.broadcasted_iota(jnp.int32, (PAY - HD, o.shape[1]), 0)
        v = jnp.where(row < 8, l, m)
        high = v.astype(BF16).astype(F32)
        rest = v - high
        mid = rest.astype(BF16).astype(F32)
        low = rest - mid
        sub = lax.rem(row, 8)
        three = jnp.where(sub == 0, high, jnp.where(sub == 1, mid, low))
        back[s, HD:PAY, cols] = three.astype(BF16)

    def lanes_of(cols):
        return pl.ds(cols.start, cols.stop - cols.start)

    def x_hop(n, ry, w):
        lanes = lanes_of(widths(ry)[w])
        return copy(
            back.at[slot((2, 1, 3)[n], ry), :, lanes],
            from_x.at[n, ry % NY, :, lanes],
            ox_s.at[n, ry % NY, w],
            ox_r.at[n, ry % NY, w],
            xm if n == 2 else xp,
        )

    def y_hop(arm, k, w):
        lanes = pl.ds(w * HALF, HALF)
        return copy(
            back.at[slot(0, (k, -k)[arm]), :, lanes],
            from_y.at[arm, k - 1, :, lanes],
            oy_s.at[arm, k - 1, w],
            oy_r.at[arm, k - 1, w],
            yp if arm == 0 else ym,
        )

    def first(ry):
        for w, cols in enumerate(widths(ry)):
            for rx, n in ((2, 0), (3, 2)):
                put(slot(rx, ry), cols, part_of(own.at[slot(rx, ry)], cols))
                go(x_hop(n, ry, w))

    def second(ry):
        for w, cols in enumerate(widths(ry)):
            x_hop(0, ry, w).wait_recv()
            s = slot(1, ry)
            put(s, cols, merge(part_of(own.at[s], cols), arrived(from_x.at[0, ry % NY], cols)))
            go(x_hop(1, ry, w))

    def joined(ry, w, cols):
        x_hop(2, ry, w).wait_recv()
        x_hop(1, ry, w).wait_recv()
        return merge(
            part_of(own.at[slot(0, ry)], cols),
            arrived(from_x.at[2, ry % NY], cols),
            arrived(from_x.at[1, ry % NY], cols),
        )

    def join(ry):
        for w, cols in enumerate(widths(ry)):
            o, l, m = joined(ry, w, cols)
            s = slot(0, ry)
            own[s, 0:HD, cols] = o
            own[s, HD : HD + 8, cols] = jnp.broadcast_to(l, (8, l.shape[1]))
            own[s, HD + 8 : PAY, cols] = jnp.broadcast_to(m, (8, m.shape[1]))

    def home(ry):
        arm, k, s = int(ry < 0), abs(ry), slot(0, ry)
        for w in range(2):
            cols = slice(w * HALF, (w + 1) * HALF)
            if k == 4 - arm:
                part = joined(ry, w, cols)
            else:
                y_hop(arm, k + 1, w).wait_recv()
                part = merge(part_of(own.at[s], cols), arrived(from_y.at[arm, k], cols))
            put(s, cols, part)
            go(y_hop(arm, k, w))

    row_on(1)
    on(2, 0)
    on(1, 1, 0, 1)
    attend(0)
    first(0)
    on(1, 1, 3, 2)
    on(3, 0, 0, 1)
    attend(1)
    first(1)
    on(3, 0, 3, 2)
    second(0)
    on(2, 1, 0, 1)
    attend(-1)
    first(-1)
    on(2, 1, 3, 2)
    second(1)
    attend(2)
    first(2)
    on(3, 1, 0, 1)
    second(-1)
    attend(-2)
    first(-2)
    on(3, 1, 3, 2)
    second(2)
    attend(-3)
    first(-3)
    second(-2)
    attend(3)
    first(3)
    on(4, 0)
    on(4, 1)
    attend(4)
    first(4)
    second(-3)
    second(3)
    join(0)
    join(1)
    second(4)
    home(-3)
    join(-1)
    join(3)
    join(2)
    join(-2)
    home(4)
    home(-2)
    home(3)
    home(-1)
    home(2)
    home(1)

    lane_i = lax.rem(lax.broadcasted_iota(jnp.int32, (1, HALF), 1), BL)
    kept = lane_i < rlen[sec, seq]

    for h in range(2):
        cols = slice(h * HALF, (h + 1) * HALF)
        y_hop(1, 1, h).wait_recv()
        y_hop(0, 1, h).wait_recv()
        o, l, _ = merge(
            part_of(mine, cols),
            part_of(own.at[0], cols),
            arrived(from_y.at[1, 0], cols),
            arrived(from_y.at[0, 0], cols),
        )
        rows = jnp.where(kept, o / l, 0.0).T
        out[0, :, 2 * h * HD : (2 * h + 1) * HD] = rows[0:BL].astype(BF16)
        out[0, :, (2 * h + 1) * HD : (2 * h + 2) * HD] = rows[BL : 2 * BL].astype(BF16)

    for done in drains:
        done()

    @pl.when(sec == 0)
    def _():
        hand.wait_send()


def shards(hidden, carried, weight, responses, prompts, prompt_lengths, response_lengths, block_prompts):
    any_space = pl.BlockSpec(memory_space=pltpu.HBM)
    scalars = pl.BlockSpec(memory_space=pltpu.SMEM)
    dma = pltpu.SemaphoreType.DMA
    vmem = pltpu.VMEM
    sems = [
        (4,),
        None,
        None,
        (4, 2),
        (4, 2),
        (2, 4, 2, 2),
        (2, 4, 2, 2),
        (3, 2),
        (3, 2),
        (2, 4, 2, NX),
        (2, 4, 2, NX),
        (3, 2),
        (3, 2),
        (2, 4, 2),
        (2, 4, 2),
        (3, NY, 2),
        (3, NY, 2),
    ]
    return pl.pallas_call(
        kernel,
        out_shape=jax.ShapeDtypeStruct((1, BL, COLS), BF16),
        in_specs=[scalars] * 3 + [any_space] * 5,
        out_specs=pl.BlockSpec(memory_space=pltpu.VMEM),
        scratch_shapes=[
            vmem((BL, 4 * WIDE), BF16),
            vmem((BL, 4 * WIDE), BF16),
            vmem((NX, BL, WIDE), BF16),
            vmem((NX, BL, WIDE), BF16),
            vmem((BL, WIDE), BF16),
            vmem((NY, DEPTH, COLS), BF16),
            vmem((NX, BL, COLS), F32),
            vmem((3, BL, COLS), F32),
            vmem((NP, TILE, 2 * HD), BF16),
            vmem((BL, 2 * HD), BF16),
            vmem((NP, PAY, TILE), BF16),
            vmem((NX * NY, HD, LANES), BF16),
            vmem((NX * NY, PAY, LANES), F32),
            vmem((PAY, LANES), F32),
            vmem((NX * NY, PAY, LANES), BF16),
            vmem((2, 4, PAY, LANES), BF16),
            vmem((3, NY, PAY, LANES), BF16),
        ]
        + [dma if s is None else dma(s) for s in sems],
        compiler_params=pltpu.CompilerParams(
            collective_id=0, has_side_effects=True, vmem_limit_bytes=63 << 20
        ),
    )(
        jnp.swapaxes(block_prompts, 1, 2),
        prompt_lengths,
        response_lengths,
        hidden,
        carried,
        weight,
        responses,
        prompts,
    )


def solution(mesh):
    placed = (
        P("sec", "seq", None),
        P("sec", "seq", None),
        P("sec", "seq", "tp"),
        P("sec", "seq", "tp"),
        P("sec", None, "seq", "tp"),
        P(),
        P(),
        P(),
    )
    return jax.shard_map(
        shards, mesh=mesh, in_specs=placed, out_specs=P("sec", "seq", "tp"), check_vma=False
    )
```

```python
import jax
import jax.numpy as jnp
from jax import lax
from jax.experimental import pallas as pl
from jax.experimental.pallas import tpu as pltpu
from jax.sharding import PartitionSpec as P

MESH = pl.DeviceIdType.MESH
HD = 128
NP = 8
TILE = 512
NX, NY = 4, 8
BL = 64
DEPTH = 160
WIDE = DEPTH * NY
COLS = 512
LANES = 256
HALF = 128
PAY = 144
SUB = DEPTH // 2
NEG = -1e30
SCALE = HD**-0.5 * 1.4426950408889634
F32 = jnp.float32
BF16 = jnp.bfloat16


def slot(rx, ry):
    return lax.rem(ry + NY, NY) * NX + rx if not isinstance(ry, int) else (ry % NY) * NX + rx


def kernel(
    bp_h,
    plen_h,
    rlen_h,
    hid_h,
    car_h,
    w_h,
    rc_h,
    kv_h,
    out,
    bp,
    plen,
    rlen,
    hid,
    handed,
    xin,
    lhs,
    transit,
    wbuf,
    pbuf,
    prec,
    kv,
    rc,
    vt,
    q,
    own,
    mine,
    back,
    from_y,
    from_x,
    local_sem,
    hand_s,
    hand_r,
    xin_s,
    xin_r,
    w_s,
    w_r,
    p_s,
    p_r,
    qy_s,
    qy_r,
    qx_s,
    qx_r,
    oy_s,
    oy_r,
    ox_s,
    ox_r,
):
    sec = lax.axis_index("sec")
    seq = lax.axis_index("seq")
    y, x = seq // NX, lax.rem(seq, NX)
    turn = 1 - 2 * sec

    def at_x(rx):
        return lax.rem(x + turn * rx + 2 * NX, NX)

    def at_y(ry):
        return lax.rem(y + turn * ry + 2 * NY, NY)

    def dev(rx, ry):
        return at_y(ry) * NX + at_x(rx)

    xp, xm, x2 = dev(1, 0), dev(-1, 0), dev(2, 0)
    yp, ym, y4 = dev(0, 1), dev(0, -1), dev(0, 4)
    y3 = (dev(0, 3), dev(0, -3))
    drains = []

    def copy(src, dst, ss, rs, where):
        return pltpu.make_async_remote_copy(
            src_ref=src,
            dst_ref=dst,
            send_sem=ss,
            recv_sem=rs,
            device_id={"seq": where},
            device_id_type=MESH,
        )

    def push(src, dst, ss, rs, where):
        c = copy(src, dst, ss, rs, where)
        c.start()
        drains.append(c.wait_send)

    def got(dst, rs):
        copy(dst, dst, rs, rs, xp).wait_recv()

    in_hid = pltpu.make_async_copy(hid_h.at[0], hid, local_sem.at[0])
    in_kv = pltpu.make_async_copy(kv_h.at[0], kv, local_sem.at[1])
    in_rc = pltpu.make_async_copy(rc_h.at[0], rc, local_sem.at[2])
    in_w = pltpu.make_async_copy(w_h.at[0], wbuf.at[y], local_sem.at[3])
    in_scalars = [
        pltpu.make_async_copy(src, dst, local_sem.at[4 + n])
        for n, (src, dst) in enumerate(((bp_h, bp), (plen_h, plen), (rlen_h, rlen)))
    ]
    in_hid.start()
    in_w.start()
    in_kv.start()
    in_rc.start()
    for c in in_scalars:
        c.start()

    barrier = pltpu.get_barrier_semaphore()
    for where in (xp, xm, x2, yp, ym, y4, *y3):
        pl.semaphore_signal(barrier, inc=1, device_id={"seq": where}, device_id_type=MESH)

    @pl.when(sec == 1)
    def _():
        pl.semaphore_signal(barrier, inc=1, device_id={"sec": 0}, device_id_type=MESH)
        pl.semaphore_wait(barrier, 8)

    @pl.when(sec == 0)
    def _():
        pl.semaphore_wait(barrier, 9)

    hand = pltpu.make_async_remote_copy(
        src_ref=car_h.at[0],
        dst_ref=handed,
        send_sem=hand_s,
        recv_sem=hand_r,
        device_id={"sec": 1},
        device_id_type=MESH,
    )

    wide = COLS // 2

    def w_part(ry, h, r):
        return wbuf.at[at_y(ry), pl.ds(r * SUB, SUB), pl.ds(h * wide, wide)]

    def w_hop(arm, k, h, r):
        sign = -1 if arm == 0 else 1
        part = w_part(sign * (k - 1), h, r)
        src = w_h.at[0, pl.ds(r * SUB, SUB), pl.ds(h * wide, wide)] if k == 1 else part
        where = yp if arm == 0 else ym
        return copy(src, part, w_s.at[arm, k - 1, h, r], w_r.at[arm, k - 1, h, r], where)

    def go(c):
        c.start()
        drains.append(c.wait_send)

    def w_on(k, h):
        for r in range(2):
            for arm in range(2):
                if k <= 4 - arm:
                    if k > 0:
                        got(w_part((-k, k)[arm], h, r), w_r.at[arm, k - 1, h, r])
                    if k < 4 - arm:
                        go(w_hop(arm, k + 1, h, r))

    w_on(0, 0)
    w_on(0, 1)

    @pl.when(sec == 0)
    def _():
        hand.start()


    rows_of = [pl.ds(r * (BL // 2), BL // 2) for r in range(2)]
    far_out = [
        copy(xin.at[at_x(2), rows], transit.at[rows], xin_s.at[2, r], xin_r.at[2, r], xp)
        for r, rows in enumerate(rows_of)
    ]
    far_on = [
        copy(transit.at[rows], lhs.at[2, rows], xin_s.at[3, r], xin_r.at[3, r], xp)
        for r, rows in enumerate(rows_of)
    ]
    near_out = [
        copy(xin.at[at_x(-1)], lhs.at[1], xin_s.at[1, 0], xin_r.at[1, 0], xm),
        copy(xin.at[at_x(1)], lhs.at[3], xin_s.at[0, 0], xin_r.at[0, 0], xp),
    ]

    def regroup(with_handed):
        def rows16(r, carry):
            rows = pl.ds(pl.multiple_of(r * 16, 16), 16)
            lane = lax.broadcasted_iota(jnp.int32, (16, 4 * DEPTH), 1)
            for g in range(2):
                parts = []
                for j in range(4):
                    cols = pl.ds(4 * DEPTH * (4 * g + j), 4 * DEPTH)
                    v = hid[rows, cols].astype(F32)
                    if with_handed:
                        v = v + handed[rows, cols].astype(F32)
                        v = v.astype(BF16).astype(F32)
                    parts.append(v)
                for xx in range(NX):
                    total = None
                    for j in range(4):
                        shift = (DEPTH * (j - xx)) % (4 * DEPTH)
                        v = parts[j] if shift == 0 else pltpu.roll(parts[j], shift, 1)
                        total = v if total is None else jnp.where(lane >= DEPTH * j, v, total)
                    xin[xx, rows, pl.ds(4 * DEPTH * g, 4 * DEPTH)] = total.astype(BF16)
            return carry

        lax.fori_loop(0, BL // 16, rows16, 0)

    def values_across(p, carry):
        vt[p, 0:HD, :] = kv[p, :, HD : 2 * HD].astype(F32).T.astype(BF16)
        vt[p, HD:PAY, :] = jnp.ones((PAY - HD, TILE), BF16)
        return carry

    in_hid.wait()

    @pl.when(sec == 0)
    def _():
        regroup(False)

    @pl.when(sec == 1)
    def _():
        hand.wait_recv()
        regroup(True)

    for c in (*far_out, *near_out):
        go(c)
    lhs[0] = xin[x]
    w_on(1, 0)
    w_on(2, 0)
    w_on(1, 1)
    for come, on_c in zip(far_out, far_on):
        come.wait_recv()
        go(on_c)
    in_kv.wait()
    lax.fori_loop(0, 3, values_across, 0)
    w_on(3, 0)
    w_on(2, 1)
    lax.fori_loop(3, 5, values_across, 0)
    w_on(4, 0)

    in_w.wait()
    in_rc.wait()
    for c in in_scalars:
        c.wait()
    for c in (*near_out, *far_on):
        c.wait_recv()

    def heads(ref, n, h):
        return ref.at[n, :, pl.ds(h * wide, wide)]

    def partial(first, h):
        rows = jnp.dot(
            lhs[first : first + 2].reshape(2 * BL, WIDE),
            wbuf[:, :, h * wide : (h + 1) * wide].reshape(WIDE, wide),
            preferred_element_type=F32,
        )
        pbuf[first : first + 2, :, h * wide : (h + 1) * wide] = rows.reshape(2, BL, wide)

    def send_partial(src, dst, h, where):
        push(heads(pbuf, src, h), heads(prec, dst, h), p_s.at[dst, h], p_r.at[dst, h], where)

    def partials(h):
        partial(2, h)
        send_partial(2, 0, h, x2)
        send_partial(3, 2, h, xm)
        partial(0, h)
        send_partial(1, 1, h, xp)

    def my_queries(h):
        cols = slice(h * wide, (h + 1) * wide)
        got(heads(prec, 2, h), p_r.at[2, h])
        got(heads(prec, 1, h), p_r.at[1, h])
        got(heads(prec, 0, h), p_r.at[0, h])
        mine_q = pbuf[0, :, cols] + prec[1, :, cols] + prec[2, :, cols] + prec[0, :, cols]
        both = jnp.concatenate([mine_q[:, 0:HD], mine_q[:, HD : 2 * HD]], axis=0)
        q[0, :, h * HALF : (h + 1) * HALF] = both.T.astype(BF16)

    def half(s, h):
        return q.at[s, :, pl.ds(h * HALF, HALF)]

    def y_out(arm, k, h, i):
        sign = -1 if arm == 0 else 1
        return copy(
            half(slot(i, sign * (k - 1)), h),
            half(slot(i, sign * k), h),
            qy_s.at[arm, k - 1, h, i],
            qy_r.at[arm, k - 1, h, i],
            yp if arm == 0 else ym,
        )

    x_side = [
        [
            copy(half(0, h), half(dst, h), qx_s.at[dst - 1, h], qx_r.at[dst - 1, h], where)
            for dst, where in ((1, xm), (3, xp), (2, x2))
        ]
        for h in range(2)
    ]

    def on(k, h, *columns):
        for i in columns or (0, 1, 3, 2):
            for arm in range(2):
                if k <= 4 - arm:
                    if k > 0:
                        y_out(arm, k, h, i).wait_recv()
                    if k < 4 - arm:
                        go(y_out(arm, k + 1, h, i))

    def row_of(h):
        my_queries(h)
        for c in x_side[h]:
            go(c)
        on(0, h, 0)

    def row_on(h):
        for c, i in zip(x_side[h], (1, 3, 2)):
            c.wait_recv()
            on(0, h, i)

    def attend(ry):
        spots = [slot(rx, ry) for rx in range(NX)]
        prompts = [bp[sec, 0, at_y(ry) * NX + at_x(rx)] for rx in range(NX)]
        valid = [plen[p] - seq * TILE for p in prompts]
        place = lax.broadcasted_iota(jnp.int32, (TILE, LANES), 0)
        scores = []
        for s, p, v in zip(spots, prompts, valid):
            raw = jnp.dot(kv[p, :, 0:HD], q[s], preferred_element_type=F32)
            scores.append(jnp.where(place < v, raw * SCALE, NEG))
        weights = []
        for s, v, score in zip(spots, valid, scores):
            peak = jnp.max(score, axis=0, keepdims=True)
            shift = jnp.where(v > 0, peak, 0.0)
            weights.append((peak, jnp.exp2(score - shift).astype(BF16)))
        for s, p, (peak, w) in zip(spots, prompts, weights):
            own[s] = jnp.dot(vt[p], w, preferred_element_type=F32)
            own[s, HD + 8 : PAY] = jnp.broadcast_to(peak, (8, LANES))

    partials(0)
    w_on(3, 1)
    lax.fori_loop(5, NP, values_across, 0)
    w_on(4, 1)
    partials(1)
    row_of(0)
    row_on(0)
    row_of(1)
    on(1, 0)

    own_s = jnp.dot(rc[:, 0:HD], q[0], preferred_element_type=F32) * SCALE
    own_t = lax.broadcasted_iota(jnp.int32, (BL, LANES), 0)
    own_i = lax.rem(lax.broadcasted_iota(jnp.int32, (BL, LANES), 1), BL)
    own_s = jnp.where(own_t <= own_i, own_s, NEG)
    own_m = jnp.max(own_s, axis=0, keepdims=True)
    own_w = jnp.exp2(own_s - own_m).astype(BF16)
    own_v = rc[:, HD : 2 * HD].astype(F32).T.astype(BF16)
    mine[0:HD] = jnp.dot(own_v, own_w, preferred_element_type=F32)
    mine[HD : HD + 8] = jnp.broadcast_to(
        jnp.sum(own_w.astype(F32), axis=0, keepdims=True), (8, LANES)
    )
    mine[HD + 8 : PAY] = jnp.broadcast_to(own_m, (8, LANES))

    def widths(ry):
        return (slice(0, HALF), slice(HALF, LANES)) if abs(ry) > 1 else (slice(0, LANES),)

    def part_of(ref, cols):
        return ref[0:HD, cols], ref[HD : HD + 1, cols], ref[HD + 8 : HD + 9, cols]

    def arrived(ref, cols):
        st = ref[HD:PAY, cols].astype(F32)
        total = st[0:1] + st[1:2] + st[2:3]
        peak = st[8:9] + st[9:10] + st[10:11]
        return ref[0:HD, cols].astype(F32), total, peak

    def merge(*parts):
        peak = parts[0][2]
        for part in parts[1:]:
            peak = jnp.maximum(peak, part[2])
        sums, total = None, None
        for o, l, m in parts:
            scale = jnp.exp2(m - peak)
            sums = o * scale if sums is None else sums + o * scale
            total = l * scale if total is None else total + l * scale
        return sums, total, peak

    def put(s, cols, part):
        o, l, m = part
        back[s, 0:HD, cols] = o.astype(BF16)
        row = lax.broadcasted_iota(jnp.int32, (PAY - HD, o.shape[1]), 0)
        v = jnp.where(row < 8, l, m)
        high = v.astype(BF16).astype(F32)
        rest = v - high
        mid = rest.astype(BF16).astype(F32)
        low = rest - mid
        sub = lax.rem(row, 8)
        three = jnp.where(sub == 0, high, jnp.where(sub == 1, mid, low))
        back[s, HD:PAY, cols] = three.astype(BF16)

    def lanes_of(cols):
        return pl.ds(cols.start, cols.stop - cols.start)

    def x_hop(n, ry, w):
        lanes = lanes_of(widths(ry)[w])
        return copy(
            back.at[slot((2, 1, 3)[n], ry), :, lanes],
            from_x.at[n, ry % NY, :, lanes],
            ox_s.at[n, ry % NY, w],
            ox_r.at[n, ry % NY, w],
            xm if n == 2 else x2 if n == 0 and abs(ry) > 2 else xp,
        )

    def y_hop(arm, k, w):
        lanes = pl.ds(w * HALF, HALF)
        return copy(
            back.at[slot(0, (k, -k)[arm]), :, lanes],
            from_y.at[arm, k - 1, :, lanes],
            oy_s.at[arm, k - 1, w],
            oy_r.at[arm, k - 1, w],
            y4 if k == 4 else y3[arm] if k == 3 else (yp, ym)[arm],
        )

    def first(ry):
        for w, cols in enumerate(widths(ry)):
            for rx, n in ((2, 0), (3, 2), (1, 1))[: 3 if abs(ry) > 2 else 2]:
                put(slot(rx, ry), cols, part_of(own.at[slot(rx, ry)], cols))
                go(x_hop(n, ry, w))

    def second(ry):
        for w, cols in enumerate(widths(ry)):
            x_hop(0, ry, w).wait_recv()
            s = slot(1, ry)
            put(s, cols, merge(part_of(own.at[s], cols), arrived(from_x.at[0, ry % NY], cols)))
            go(x_hop(1, ry, w))

    def joined(ry, w, cols):
        hops = (2, 1, 0) if abs(ry) > 2 else (2, 1)
        for n in hops:
            x_hop(n, ry, w).wait_recv()
        return merge(
            part_of(own.at[slot(0, ry)], cols),
            *[arrived(from_x.at[n, ry % NY], cols) for n in hops],
        )

    def join(ry):
        for w, cols in enumerate(widths(ry)):
            o, l, m = joined(ry, w, cols)
            s = slot(0, ry)
            own[s, 0:HD, cols] = o
            own[s, HD : HD + 8, cols] = jnp.broadcast_to(l, (8, l.shape[1]))
            own[s, HD + 8 : PAY, cols] = jnp.broadcast_to(m, (8, m.shape[1]))

    def home(ry):
        arm, k, s = int(ry < 0), abs(ry), slot(0, ry)
        for w in range(2):
            cols = slice(w * HALF, (w + 1) * HALF)
            if k >= 2:
                part = joined(ry, w, cols)
            else:
                y_hop(arm, k + 1, w).wait_recv()
                part = merge(part_of(own.at[s], cols), arrived(from_y.at[arm, k], cols))
            put(s, cols, part)
            go(y_hop(arm, k, w))

    row_on(1)
    on(2, 0)
    on(1, 1, 0, 1)
    attend(0)
    first(0)
    on(1, 1, 3, 2)
    on(3, 0, 0, 1)
    attend(1)
    first(1)
    on(3, 0, 3, 2)
    second(0)
    on(2, 1, 0, 1)
    attend(-1)
    first(-1)
    on(2, 1, 3, 2)
    second(1)
    attend(2)
    first(2)
    on(3, 1, 0, 1)
    second(-1)
    attend(-2)
    first(-2)
    on(3, 1, 3, 2)
    second(2)
    attend(-3)
    first(-3)
    second(-2)
    attend(3)
    first(3)
    on(4, 0)
    on(4, 1)
    attend(4)
    first(4)
    join(0)
    join(1)
    home(-3)
    home(3)
    home(-2)
    home(2)
    home(4)
    join(-1)
    home(-1)
    home(1)

    lane_i = lax.rem(lax.broadcasted_iota(jnp.int32, (1, HALF), 1), BL)
    kept = lane_i < rlen[sec, seq]

    for h in range(2):
        cols = slice(h * HALF, (h + 1) * HALF)
        y_hop(1, 1, h).wait_recv()
        y_hop(0, 1, h).wait_recv()
        y_hop(0, 3, h).wait_recv()
        y_hop(1, 3, h).wait_recv()
        y_hop(0, 4, h).wait_recv()
        o, l, _ = merge(
            part_of(mine, cols),
            part_of(own.at[0], cols),
            arrived(from_y.at[1, 0], cols),
            arrived(from_y.at[0, 0], cols),
            arrived(from_y.at[0, 2], cols),
            arrived(from_y.at[1, 2], cols),
            arrived(from_y.at[0, 3], cols),
        )
        rows = jnp.where(kept, o / l, 0.0).T
        out[0, :, 2 * h * HD : (2 * h + 1) * HD] = rows[0:BL].astype(BF16)
        out[0, :, (2 * h + 1) * HD : (2 * h + 2) * HD] = rows[BL : 2 * BL].astype(BF16)

    for done in drains:
        done()

    @pl.when(sec == 0)
    def _():
        hand.wait_send()


def shards(hidden, carried, weight, responses, prompts, prompt_lengths, response_lengths, block_prompts):
    any_space = pl.BlockSpec(memory_space=pltpu.HBM)
    dma = pltpu.SemaphoreType.DMA
    vmem = pltpu.VMEM
    sems = [
        (7,),
        None,
        None,
        (4, 2),
        (4, 2),
        (2, 4, 2, 2),
        (2, 4, 2, 2),
        (3, 2),
        (3, 2),
        (2, 4, 2, NX),
        (2, 4, 2, NX),
        (3, 2),
        (3, 2),
        (2, 4, 2),
        (2, 4, 2),
        (3, NY, 2),
        (3, NY, 2),
    ]
    return pl.pallas_call(
        kernel,
        out_shape=jax.ShapeDtypeStruct((1, BL, COLS), BF16),
        in_specs=[any_space] * 8,
        out_specs=pl.BlockSpec(memory_space=pltpu.VMEM),
        scratch_shapes=[
            pltpu.SMEM((2, 1, NX * NY), jnp.int32),
            pltpu.SMEM((NP,), jnp.int32),
            pltpu.SMEM((2, NX * NY), jnp.int32),
            vmem((BL, 4 * WIDE), BF16),
            vmem((BL, 4 * WIDE), BF16),
            vmem((NX, BL, WIDE), BF16),
            vmem((NX, BL, WIDE), BF16),
            vmem((BL, WIDE), BF16),
            vmem((NY, DEPTH, COLS), BF16),
            vmem((NX, BL, COLS), F32),
            vmem((3, BL, COLS), F32),
            vmem((NP, TILE, 2 * HD), BF16),
            vmem((BL, 2 * HD), BF16),
            vmem((NP, PAY, TILE), BF16),
            vmem((NX * NY, HD, LANES), BF16),
            vmem((NX * NY, PAY, LANES), F32),
            vmem((PAY, LANES), F32),
            vmem((NX * NY, PAY, LANES), BF16),
            vmem((2, 4, PAY, LANES), BF16),
            vmem((3, NY, PAY, LANES), BF16),
        ]
        + [dma if s is None else dma(s) for s in sems],
        compiler_params=pltpu.CompilerParams(
            collective_id=0, has_side_effects=True, vmem_limit_bytes=63 << 20
        ),
    )(
        jnp.swapaxes(block_prompts, 1, 2),
        prompt_lengths,
        response_lengths,
        hidden,
        carried,
        weight,
        responses,
        prompts,
    )


def solution(mesh):
    placed = (
        P("sec", "seq", None),
        P("sec", "seq", None),
        P("sec", "seq", "tp"),
        P("sec", "seq", "tp"),
        P("sec", None, "seq", "tp"),
        P(),
        P(),
        P(),
    )
    return jax.shard_map(
        shards, mesh=mesh, in_specs=placed, out_specs=P("sec", "seq", "tp"), check_vma=False
    )
```

```python
import jax
import jax.numpy as jnp
from jax import lax
from jax.experimental import pallas as pl
from jax.experimental.pallas import tpu as pltpu
from jax.sharding import PartitionSpec as P

MESH = pl.DeviceIdType.MESH
HD = 128
NP = 8
TILE = 512
NX, NY = 4, 8
BL = 64
DEPTH = 160
WIDE = DEPTH * NY
COLS = 512
LANES = 256
HALF = 128
PAY = 144
SUB = DEPTH // 2
NEG = -1e30
SCALE = HD**-0.5 * 1.4426950408889634
F32 = jnp.float32
BF16 = jnp.bfloat16


def slot(rx, ry):
    return lax.rem(ry + NY, NY) * NX + rx if not isinstance(ry, int) else (ry % NY) * NX + rx


def kernel(
    bp_h,
    plen_h,
    rlen_h,
    hid_h,
    car_h,
    w_h,
    rc_h,
    kv_h,
    out,
    bp,
    plen,
    rlen,
    hid,
    handed,
    xin,
    lhs,
    transit,
    wbuf,
    pbuf,
    prec,
    kv,
    rc,
    vt,
    q,
    own,
    mine,
    back,
    from_y,
    from_x,
    local_sem,
    hand_s,
    hand_r,
    xin_s,
    xin_r,
    w_s,
    w_r,
    p_s,
    p_r,
    qy_s,
    qy_r,
    qx_s,
    qx_r,
    oy_s,
    oy_r,
    ox_s,
    ox_r,
):
    sec = lax.axis_index("sec")
    seq = lax.axis_index("seq")
    y, x = seq // NX, lax.rem(seq, NX)
    turn = 1 - 2 * sec

    def at_x(rx):
        return lax.rem(x + turn * rx + 2 * NX, NX)

    def at_y(ry):
        return lax.rem(y + turn * ry + 2 * NY, NY)

    def dev(rx, ry):
        return at_y(ry) * NX + at_x(rx)

    xp, xm, x2 = dev(1, 0), dev(-1, 0), dev(2, 0)
    yp, ym, y4 = dev(0, 1), dev(0, -1), dev(0, 4)
    y3 = (dev(0, 3), dev(0, -3))
    drains = []

    def copy(src, dst, ss, rs, where):
        return pltpu.make_async_remote_copy(
            src_ref=src,
            dst_ref=dst,
            send_sem=ss,
            recv_sem=rs,
            device_id={"seq": where},
            device_id_type=MESH,
        )

    def push(src, dst, ss, rs, where):
        c = copy(src, dst, ss, rs, where)
        c.start()
        drains.append(c.wait_send)

    def got(dst, rs):
        copy(dst, dst, rs, rs, xp).wait_recv()

    in_hid = pltpu.make_async_copy(hid_h.at[0], hid, local_sem.at[0])
    in_kv = pltpu.make_async_copy(kv_h.at[0], kv, local_sem.at[1])
    in_rc = pltpu.make_async_copy(rc_h.at[0], rc, local_sem.at[2])
    in_w = pltpu.make_async_copy(w_h.at[0], wbuf.at[y], local_sem.at[3])
    in_scalars = [
        pltpu.make_async_copy(src, dst, local_sem.at[4 + n])
        for n, (src, dst) in enumerate(((bp_h, bp), (plen_h, plen), (rlen_h, rlen)))
    ]
    in_hid.start()
    in_w.start()
    in_kv.start()
    in_rc.start()
    for c in in_scalars:
        c.start()

    barrier = pltpu.get_barrier_semaphore()
    for where in (xp, xm, x2, yp, ym, y4, *y3):
        pl.semaphore_signal(barrier, inc=1, device_id={"seq": where}, device_id_type=MESH)

    @pl.when(sec == 1)
    def _():
        pl.semaphore_signal(barrier, inc=1, device_id={"sec": 0}, device_id_type=MESH)
        pl.semaphore_wait(barrier, 8)

    @pl.when(sec == 0)
    def _():
        pl.semaphore_wait(barrier, 9)

    hand = pltpu.make_async_remote_copy(
        src_ref=car_h.at[0],
        dst_ref=handed,
        send_sem=hand_s,
        recv_sem=hand_r,
        device_id={"sec": 1},
        device_id_type=MESH,
    )

    wide = COLS // 2

    def w_part(ry, h, r):
        return wbuf.at[at_y(ry), pl.ds(r * SUB, SUB), pl.ds(h * wide, wide)]

    def w_hop(arm, k, h, r):
        sign = -1 if arm == 0 else 1
        part = w_part(sign * (k - 1), h, r)
        src = w_h.at[0, pl.ds(r * SUB, SUB), pl.ds(h * wide, wide)] if k == 1 else part
        where = yp if arm == 0 else ym
        return copy(src, part, w_s.at[arm, k - 1, h, r], w_r.at[arm, k - 1, h, r], where)

    def go(c):
        c.start()
        drains.append(c.wait_send)

    def w_on(k, h):
        for r in range(2):
            for arm in range(2):
                if k <= 4 - arm:
                    if k > 0:
                        got(w_part((-k, k)[arm], h, r), w_r.at[arm, k - 1, h, r])
                    if k < 4 - arm:
                        go(w_hop(arm, k + 1, h, r))

    w_on(0, 0)
    w_on(0, 1)

    @pl.when(sec == 0)
    def _():
        hand.start()


    rows_of = [pl.ds(r * (BL // 2), BL // 2) for r in range(2)]
    far_out = [
        copy(xin.at[at_x(2), rows], transit.at[rows], xin_s.at[2, r], xin_r.at[2, r], xp)
        for r, rows in enumerate(rows_of)
    ]
    far_on = [
        copy(transit.at[rows], lhs.at[2, rows], xin_s.at[3, r], xin_r.at[3, r], xp)
        for r, rows in enumerate(rows_of)
    ]
    near_out = [
        copy(xin.at[at_x(-1)], lhs.at[1], xin_s.at[1, 0], xin_r.at[1, 0], xm),
        copy(xin.at[at_x(1)], lhs.at[3], xin_s.at[0, 0], xin_r.at[0, 0], xp),
    ]

    def regroup(with_handed):
        def rows16(r, carry):
            rows = pl.ds(pl.multiple_of(r * 16, 16), 16)
            lane = lax.broadcasted_iota(jnp.int32, (16, 4 * DEPTH), 1)
            for g in range(2):
                parts = []
                for j in range(4):
                    cols = pl.ds(4 * DEPTH * (4 * g + j), 4 * DEPTH)
                    v = hid[rows, cols].astype(F32)
                    if with_handed:
                        v = v + handed[rows, cols].astype(F32)
                        v = v.astype(BF16).astype(F32)
                    parts.append(v)
                for xx in range(NX):
                    total = None
                    for j in range(4):
                        shift = (DEPTH * (j - xx)) % (4 * DEPTH)
                        v = parts[j] if shift == 0 else pltpu.roll(parts[j], shift, 1)
                        total = v if total is None else jnp.where(lane >= DEPTH * j, v, total)
                    xin[xx, rows, pl.ds(4 * DEPTH * g, 4 * DEPTH)] = total.astype(BF16)
            return carry

        lax.fori_loop(0, BL // 16, rows16, 0)

    def values_across(p, carry):
        vt[p, 0:HD, :] = kv[p, :, HD : 2 * HD].astype(F32).T.astype(BF16)
        vt[p, HD:PAY, :] = jnp.ones((PAY - HD, TILE), BF16)
        return carry

    in_hid.wait()

    @pl.when(sec == 0)
    def _():
        regroup(False)

    @pl.when(sec == 1)
    def _():
        hand.wait_recv()
        regroup(True)

    for c in (*far_out, *near_out):
        go(c)
    lhs[0] = xin[x]
    w_on(1, 0)
    w_on(2, 0)
    w_on(1, 1)
    for come, on_c in zip(far_out, far_on):
        come.wait_recv()
        go(on_c)
    in_kv.wait()
    lax.fori_loop(0, 3, values_across, 0)
    w_on(3, 0)
    w_on(2, 1)
    lax.fori_loop(3, 5, values_across, 0)
    w_on(4, 0)

    in_w.wait()
    in_rc.wait()
    for c in in_scalars:
        c.wait()
    for c in (*near_out, *far_on):
        c.wait_recv()

    def heads(ref, n, h):
        return ref.at[n, :, pl.ds(h * wide, wide)]

    def partial(first, h):
        rows = jnp.dot(
            lhs[first : first + 2].reshape(2 * BL, WIDE),
            wbuf[:, :, h * wide : (h + 1) * wide].reshape(WIDE, wide),
            preferred_element_type=F32,
        )
        pbuf[first : first + 2, :, h * wide : (h + 1) * wide] = rows.reshape(2, BL, wide)

    def send_partial(src, dst, h, where):
        push(heads(pbuf, src, h), heads(prec, dst, h), p_s.at[dst, h], p_r.at[dst, h], where)

    def partials(h):
        partial(2, h)
        send_partial(2, 0, h, x2)
        send_partial(3, 2, h, xm)
        partial(0, h)
        send_partial(1, 1, h, xp)

    def my_queries(h):
        cols = slice(h * wide, (h + 1) * wide)
        got(heads(prec, 2, h), p_r.at[2, h])
        got(heads(prec, 1, h), p_r.at[1, h])
        got(heads(prec, 0, h), p_r.at[0, h])
        mine_q = pbuf[0, :, cols] + prec[1, :, cols] + prec[2, :, cols] + prec[0, :, cols]
        both = jnp.concatenate([mine_q[:, 0:HD], mine_q[:, HD : 2 * HD]], axis=0)
        q[0, :, h * HALF : (h + 1) * HALF] = both.T.astype(BF16)

    def half(s, h):
        return q.at[s, :, pl.ds(h * HALF, HALF)]

    def y_out(arm, k, h, i):
        sign = -1 if arm == 0 else 1
        return copy(
            half(slot(i, sign * (k - 1)), h),
            half(slot(i, sign * k), h),
            qy_s.at[arm, k - 1, h, i],
            qy_r.at[arm, k - 1, h, i],
            yp if arm == 0 else ym,
        )

    x_side = [
        [
            copy(half(0, h), half(dst, h), qx_s.at[dst - 1, h], qx_r.at[dst - 1, h], where)
            for dst, where in ((1, xm), (3, xp), (2, x2))
        ]
        for h in range(2)
    ]

    def on(k, h, *columns):
        for i in columns or (0, 1, 3, 2):
            for arm in range(2):
                if k <= 4 - arm:
                    if k > 0:
                        y_out(arm, k, h, i).wait_recv()
                    if k < 4 - arm:
                        go(y_out(arm, k + 1, h, i))

    def row_of(h):
        my_queries(h)
        for c in x_side[h]:
            go(c)
        on(0, h, 0)

    def row_on(h):
        for c, i in zip(x_side[h], (1, 3, 2)):
            c.wait_recv()
            on(0, h, i)

    def attend(ry):
        spots = [slot(rx, ry) for rx in range(NX)]
        prompts = [bp[sec, 0, at_y(ry) * NX + at_x(rx)] for rx in range(NX)]
        valid = [plen[p] - seq * TILE for p in prompts]
        place = lax.broadcasted_iota(jnp.int32, (TILE, LANES), 0)
        scores = []
        for s, p, v in zip(spots, prompts, valid):
            raw = jnp.dot(kv[p, :, 0:HD], q[s], preferred_element_type=F32)
            scores.append(jnp.where(place < v, raw * SCALE, NEG))
        weights = []
        for s, v, score in zip(spots, valid, scores):
            peak = jnp.max(score, axis=0, keepdims=True)
            shift = jnp.where(v > 0, peak, 0.0)
            weights.append((peak, jnp.exp2(score - shift).astype(BF16)))
        for s, p, (peak, w) in zip(spots, prompts, weights):
            own[s] = jnp.dot(vt[p], w, preferred_element_type=F32)
            own[s, HD + 8 : PAY] = jnp.broadcast_to(peak, (8, LANES))

    partials(0)
    w_on(3, 1)
    lax.fori_loop(5, NP, values_across, 0)
    w_on(4, 1)
    partials(1)
    row_of(0)
    row_on(0)
    row_of(1)
    on(1, 0)

    own_s = jnp.dot(rc[:, 0:HD], q[0], preferred_element_type=F32) * SCALE
    own_t = lax.broadcasted_iota(jnp.int32, (BL, LANES), 0)
    own_i = lax.rem(lax.broadcasted_iota(jnp.int32, (BL, LANES), 1), BL)
    own_s = jnp.where(own_t <= own_i, own_s, NEG)
    own_m = jnp.max(own_s, axis=0, keepdims=True)
    own_w = jnp.exp2(own_s - own_m).astype(BF16)
    own_v = rc[:, HD : 2 * HD].astype(F32).T.astype(BF16)
    mine[0:HD] = jnp.dot(own_v, own_w, preferred_element_type=F32)
    mine[HD : HD + 8] = jnp.broadcast_to(
        jnp.sum(own_w.astype(F32), axis=0, keepdims=True), (8, LANES)
    )
    mine[HD + 8 : PAY] = jnp.broadcast_to(own_m, (8, LANES))

    def widths(ry):
        return (slice(0, HALF), slice(HALF, LANES)) if abs(ry) > 1 else (slice(0, LANES),)

    def part_of(ref, cols):
        return ref[0:HD, cols], ref[HD : HD + 1, cols], ref[HD + 8 : HD + 9, cols]

    def arrived(ref, cols):
        st = ref[HD:PAY, cols].astype(F32)
        total = st[0:1] + st[1:2] + st[2:3]
        peak = st[8:9] + st[9:10] + st[10:11]
        return ref[0:HD, cols].astype(F32), total, peak

    def merge(*parts):
        peak = parts[0][2]
        for part in parts[1:]:
            peak = jnp.maximum(peak, part[2])
        sums, total = None, None
        for o, l, m in parts:
            scale = jnp.exp2(m - peak)
            sums = o * scale if sums is None else sums + o * scale
            total = l * scale if total is None else total + l * scale
        return sums, total, peak

    def put(s, cols, part):
        o, l, m = part
        back[s, 0:HD, cols] = o.astype(BF16)
        row = lax.broadcasted_iota(jnp.int32, (PAY - HD, o.shape[1]), 0)
        v = jnp.where(row < 8, l, m)
        high = v.astype(BF16).astype(F32)
        rest = v - high
        mid = rest.astype(BF16).astype(F32)
        low = rest - mid
        sub = lax.rem(row, 8)
        three = jnp.where(sub == 0, high, jnp.where(sub == 1, mid, low))
        back[s, HD:PAY, cols] = three.astype(BF16)

    def lanes_of(cols):
        return pl.ds(cols.start, cols.stop - cols.start)

    def x_hop(n, ry, w):
        lanes = lanes_of(widths(ry)[w])
        return copy(
            back.at[slot((2, 1, 3)[n], ry), :, lanes],
            from_x.at[n, ry % NY, :, lanes],
            ox_s.at[n, ry % NY, w],
            ox_r.at[n, ry % NY, w],
            xm if n == 2 else x2 if n == 0 and abs(ry) > 1 else xp,
        )

    def y_hop(arm, k, w):
        lanes = pl.ds(w * HALF, HALF)
        return copy(
            back.at[slot(0, (k, -k)[arm]), :, lanes],
            from_y.at[arm, k - 1, :, lanes],
            oy_s.at[arm, k - 1, w],
            oy_r.at[arm, k - 1, w],
            y4 if k == 4 else y3[arm] if k == 3 else (yp, ym)[arm],
        )

    def first(ry):
        for w, cols in enumerate(widths(ry)):
            for rx, n in ((2, 0), (3, 2), (1, 1))[: 3 if abs(ry) > 1 else 2]:
                put(slot(rx, ry), cols, part_of(own.at[slot(rx, ry)], cols))
                go(x_hop(n, ry, w))

    def second(ry):
        for w, cols in enumerate(widths(ry)):
            x_hop(0, ry, w).wait_recv()
            s = slot(1, ry)
            put(s, cols, merge(part_of(own.at[s], cols), arrived(from_x.at[0, ry % NY], cols)))
            go(x_hop(1, ry, w))

    def joined(ry, w, cols):
        hops = (2, 1, 0) if abs(ry) > 1 else (2, 1)
        for n in hops:
            x_hop(n, ry, w).wait_recv()
        return merge(
            part_of(own.at[slot(0, ry)], cols),
            *[arrived(from_x.at[n, ry % NY], cols) for n in hops],
        )

    def join(ry):
        for w, cols in enumerate(widths(ry)):
            o, l, m = joined(ry, w, cols)
            s = slot(0, ry)
            own[s, 0:HD, cols] = o
            own[s, HD : HD + 8, cols] = jnp.broadcast_to(l, (8, l.shape[1]))
            own[s, HD + 8 : PAY, cols] = jnp.broadcast_to(m, (8, m.shape[1]))

    def home(ry):
        arm, k, s = int(ry < 0), abs(ry), slot(0, ry)
        for w in range(2):
            cols = slice(w * HALF, (w + 1) * HALF)
            if k >= 2:
                part = joined(ry, w, cols)
            else:
                y_hop(arm, k + 1, w).wait_recv()
                part = merge(part_of(own.at[s], cols), arrived(from_y.at[arm, k], cols))
            put(s, cols, part)
            go(y_hop(arm, k, w))

    row_on(1)
    on(2, 0)
    on(1, 1, 0, 1)
    attend(0)
    first(0)
    on(1, 1, 3, 2)
    on(3, 0, 0, 1)
    attend(1)
    first(1)
    on(3, 0, 3, 2)
    second(0)
    on(2, 1, 0, 1)
    attend(-1)
    first(-1)
    on(2, 1, 3, 2)
    second(1)
    attend(2)
    first(2)
    on(3, 1, 0, 1)
    second(-1)
    attend(-2)
    first(-2)
    on(3, 1, 3, 2)
    attend(-3)
    first(-3)
    attend(3)
    first(3)
    on(4, 0)
    on(4, 1)
    attend(4)
    first(4)
    join(0)
    join(1)
    home(-3)
    home(3)
    home(-2)
    home(2)
    home(4)
    join(-1)
    home(-1)
    home(1)

    lane_i = lax.rem(lax.broadcasted_iota(jnp.int32, (1, HALF), 1), BL)
    kept = lane_i < rlen[sec, seq]

    for h in range(2):
        cols = slice(h * HALF, (h + 1) * HALF)
        y_hop(1, 1, h).wait_recv()
        y_hop(0, 1, h).wait_recv()
        y_hop(0, 3, h).wait_recv()
        y_hop(1, 3, h).wait_recv()
        y_hop(0, 4, h).wait_recv()
        o, l, _ = merge(
            part_of(mine, cols),
            part_of(own.at[0], cols),
            arrived(from_y.at[1, 0], cols),
            arrived(from_y.at[0, 0], cols),
            arrived(from_y.at[0, 2], cols),
            arrived(from_y.at[1, 2], cols),
            arrived(from_y.at[0, 3], cols),
        )
        rows = jnp.where(kept, o / l, 0.0).T
        out[0, :, 2 * h * HD : (2 * h + 1) * HD] = rows[0:BL].astype(BF16)
        out[0, :, (2 * h + 1) * HD : (2 * h + 2) * HD] = rows[BL : 2 * BL].astype(BF16)

    for done in drains:
        done()

    @pl.when(sec == 0)
    def _():
        hand.wait_send()


def shards(hidden, carried, weight, responses, prompts, prompt_lengths, response_lengths, block_prompts):
    any_space = pl.BlockSpec(memory_space=pltpu.HBM)
    dma = pltpu.SemaphoreType.DMA
    vmem = pltpu.VMEM
    sems = [
        (7,),
        None,
        None,
        (4, 2),
        (4, 2),
        (2, 4, 2, 2),
        (2, 4, 2, 2),
        (3, 2),
        (3, 2),
        (2, 4, 2, NX),
        (2, 4, 2, NX),
        (3, 2),
        (3, 2),
        (2, 4, 2),
        (2, 4, 2),
        (3, NY, 2),
        (3, NY, 2),
    ]
    return pl.pallas_call(
        kernel,
        out_shape=jax.ShapeDtypeStruct((1, BL, COLS), BF16),
        in_specs=[any_space] * 8,
        out_specs=pl.BlockSpec(memory_space=pltpu.VMEM),
        scratch_shapes=[
            pltpu.SMEM((2, 1, NX * NY), jnp.int32),
            pltpu.SMEM((NP,), jnp.int32),
            pltpu.SMEM((2, NX * NY), jnp.int32),
            vmem((BL, 4 * WIDE), BF16),
            vmem((BL, 4 * WIDE), BF16),
            vmem((NX, BL, WIDE), BF16),
            vmem((NX, BL, WIDE), BF16),
            vmem((BL, WIDE), BF16),
            vmem((NY, DEPTH, COLS), BF16),
            vmem((NX, BL, COLS), F32),
            vmem((3, BL, COLS), F32),
            vmem((NP, TILE, 2 * HD), BF16),
            vmem((BL, 2 * HD), BF16),
            vmem((NP, PAY, TILE), BF16),
            vmem((NX * NY, HD, LANES), BF16),
            vmem((NX * NY, PAY, LANES), F32),
            vmem((PAY, LANES), F32),
            vmem((NX * NY, PAY, LANES), BF16),
            vmem((2, 4, PAY, LANES), BF16),
            vmem((3, NY, PAY, LANES), BF16),
        ]
        + [dma if s is None else dma(s) for s in sems],
        compiler_params=pltpu.CompilerParams(
            collective_id=0, has_side_effects=True, vmem_limit_bytes=63 << 20
        ),
    )(
        jnp.swapaxes(block_prompts, 1, 2),
        prompt_lengths,
        response_lengths,
        hidden,
        carried,
        weight,
        responses,
        prompts,
    )


def solution(mesh):
    placed = (
        P("sec", "seq", None),
        P("sec", "seq", None),
        P("sec", "seq", "tp"),
        P("sec", "seq", "tp"),
        P("sec", None, "seq", "tp"),
        P(),
        P(),
        P(),
    )
    return jax.shard_map(
        shards, mesh=mesh, in_specs=placed, out_specs=P("sec", "seq", "tp"), check_vma=False
    )
```
